512 devices in a mesh: mp: 32 (over z, y_lo), dp: 16 (over x, y_hi, core).
Axes of the slice: x: 4, y: 8 (y_hi: 2, y_lo: 4; y = y_hi * 4 + y_lo), z: 8, core: 2. Of those that a mesh axis runs over, the one named last changes fastest.
Arguments:
- forward_fields: bfloat16 [16, 4, 65536], P(None, None, 'mp'), may hold values from -6 to 6
- adjoint_fields: bfloat16 [64, 4, 65536], P(None, None, 'mp'), may hold values from -6 to 6
- data_rec: int32 [3072], P('dp'), may hold values from 0 to 63
- data_freq: int32 [3072], P('dp'), may hold values from 0 to 15
- data_coef: float32 [3072, 4], P('dp'), may hold values from -6 to 6
- residual_cols: bfloat16 [3072, 256], P('dp'), may hold values from -6 to 6
Outputs:
- data_update: bfloat16 [3072, 256], P('dp')
- model_update: float32 [65536, 256], P(('mp', 'dp'))
The draws below stay inside these ranges and needn't reach their ends.
All inputs are finite; a program needn't handle non-finite values.
Results may differ from the reference program's by a relative error of at most 0.0075.
Values may be sent and summed in bfloat16 or wider, within the bound.
No kernel may reach another device: no remote copies, remote signals or barrier semaphores. Data moves between devices by JAX's collectives and lax.ppermute only.
A program may use at most 64 MiB of HBM per device.

```python
import math
import jax
import jax.numpy as jnp
from jax import lax

DATA_DEV = 192
GRID_COLS = 128
RHS = 256
NREC = 64
NFREQ = 16
KC = 4
SWEEPS = 2
GRID_ROWS = 512
NCELL = 65536
NDATA = 3072


def place_ends(values, stream_key, smallest, largest):
    index_at = [jax.random.randint(jax.random.fold_in(stream_key, axis), (), 0, length) for axis, length in enumerate(values.shape)]
    main_axis = values.shape.index(max(values.shape))
    next_to = index_at[:main_axis] + [(index_at[main_axis] + 1) % values.shape[main_axis]] + index_at[main_axis + 1:]
    return values.at[tuple(index_at)].set(smallest).at[tuple(next_to)].set(largest)


def block_scale(key, shape, split, least, high):
    factor_of, own = 1.0, jax.random.fold_in(key, 6)
    for axis_at, shards_of in split:
        heights = jnp.exp(jax.random.uniform(jax.random.fold_in(own, axis_at), (shards_of,), jnp.float32, least / len(split), high / len(split)))
        factor_of = factor_of * jnp.repeat(heights, shape[axis_at] // shards_of).reshape([-1 if axis == axis_at else 1 for axis in range(len(shape))])
    return factor_of


def scatter_about(own_key, dims, width, reach, split=(), kind=jnp.bfloat16):
    values = jax.random.normal(own_key, dims, jnp.float32) * width
    if len(split) > 0:
        values = block_scale(own_key, dims, split, -0.22, 0.18) * values
    return jnp.clip(values, min=-reach, max=reach).astype(kind)


def setup_inputs(seed: int = 0) -> dict:
    key_of = jax.random.split(jax.random.key(seed), 7)
    return {
        "forward_fields": scatter_about(key_of[0], (NFREQ, KC, NCELL), 1.0, 6.0, ((2, 32),)),
        "adjoint_fields": scatter_about(key_of[1], (NREC, KC, NCELL), 1.0, 6.0, ((2, 32),)),
        "data_rec": place_ends(jax.random.randint(key_of[2], (NDATA,), 0, NREC), jax.random.fold_in(key_of[2], 1), 0, NREC - 1).astype(jnp.int32),
        "data_freq": place_ends(jax.random.randint(key_of[3], (NDATA,), 0, NFREQ), jax.random.fold_in(key_of[3], 1), 0, NFREQ - 1).astype(jnp.int32),
        "data_coef": scatter_about(key_of[4], (NDATA, KC), 1.0, 6.0, ((0, 16),), jnp.float32),
        "residual_cols": scatter_about(key_of[5], (NDATA, RHS), 1.0, 6.0, ((0, 16),)),
    }


def smooth_grid(field):
    for sweep in range(SWEEPS):
        padded = jnp.pad(field, ((0, 0), (1, 1), (1, 1)))
        beside_all = padded[:, :-2, 1:-1] + padded[:, 2:, 1:-1] + padded[:, 1:-1, :-2] + padded[:, 1:-1, 2:]
        field = field + 0.2 * (beside_all - 4.0 * field)
    return field

def reference(forward_fields, adjoint_fields, data_rec, data_freq, data_coef, residual_cols):
    blocks = NDATA // DATA_DEV

    def one_block(index):
        start = index * DATA_DEV
        recs = lax.dynamic_slice_in_dim(data_rec, start, DATA_DEV, 0)
        freqs = lax.dynamic_slice_in_dim(data_freq, start, DATA_DEV, 0)
        coefs = lax.dynamic_slice_in_dim(data_coef, start, DATA_DEV, 0)
        adjoint = adjoint_fields[recs].astype(jnp.float32)
        forward = forward_fields[freqs].astype(jnp.float32)
        sens = (0.5 * lax.optimization_barrier(jnp.sum(coefs[:, :, None] * adjoint * forward, axis=1))).astype(jnp.bfloat16)
        grid = sens.astype(jnp.float32).reshape(DATA_DEV, GRID_ROWS, GRID_COLS)
        smooth = smooth_grid(grid).reshape(DATA_DEV, NCELL).astype(jnp.bfloat16)
        return (sens, smooth)
    sens_all, smooth_all = lax.map(one_block, jnp.arange(blocks, dtype=jnp.int32))
    sens_all = sens_all.reshape(NDATA, NCELL)
    smooth_all = smooth_all.reshape(NDATA, NCELL)
    back = lax.dot_general(sens_all, residual_cols, (((0,), (0,)), ((), ())), preferred_element_type=jnp.float32)
    gram_prod = jnp.dot(smooth_all.astype(jnp.float32), back, precision=lax.Precision.HIGHEST) / NCELL
    data_update = (gram_prod + residual_cols.astype(jnp.float32)).astype(jnp.bfloat16)
    model_update = lax.dot_general(smooth_all, data_update, (((0,), (0,)), ((), ())), preferred_element_type=jnp.float32)
    return (data_update, model_update / math.sqrt(NDATA))
```

```python
import functools
import math

import jax
import jax.numpy as jnp
from jax import lax
from jax.experimental import pallas as pl
from jax.experimental.pallas import tpu as pltpu
from jax.sharding import PartitionSpec as P

BF, F32 = jnp.bfloat16, jnp.float32
COLS = 128
HALO = 2 * COLS
NREC, NFREQ, KC = 64, 16, 4
FK, RK = NFREQ * KC, NREC * KC
DATA, RHS, BLOCKS, SLABS = 192, 256, 16, 32
NDATA, CELLS = DATA * BLOCKS, 2048
Q = RHS // BLOCKS
TILES = NDATA // 128
GRID_ROWS = CELLS // COLS
NT = (((1,), (1,)), ((), ()))


def whole(n):
    return [pl.BlockSpec(memory_space=pltpu.VMEM)] * n


def pack_kernel(res_ref, coef_ref, rec_ref, freq_ref, out_ref, big, small):
    odd = lax.rem(lax.axis_index("dp"), 2) == 1
    big[...] = jnp.zeros_like(big)
    small[...] = jnp.zeros_like(small)
    big[0:DATA, :] = res_ref[...].astype(F32)
    small[0:DATA, 0:KC] = coef_ref[...]
    res = jnp.transpose(big[...])
    coef = jnp.transpose(small[...])[0:8]
    hi = coef.astype(BF).astype(F32)
    lo = coef - hi
    pad = jnp.zeros((1, 64), F32)
    rec = jnp.concatenate([rec_ref[...].astype(F32), pad], axis=1)
    freq = jnp.concatenate([freq_ref[...].astype(F32), pad], axis=1)
    row = lax.broadcasted_iota(jnp.int32, (8, 256), 0)
    head = jnp.where(row < KC, hi, pltpu.roll(lo, KC, 0))
    index = jnp.where(row == 0, rec, jnp.where(row == 1, freq, 0.0))
    side = jnp.concatenate([head, index], axis=0)

    def place(v):
        tail = v[:, 128:256]
        tail = jnp.where(odd, pltpu.roll(tail, 64, 1), tail)
        return jnp.concatenate([v[:, 0:128], tail], axis=1).astype(BF)

    res = place(res)
    side = place(side)
    for b in range(BLOCKS):
        out_ref[b, 0:Q, :] = res[b * Q : (b + 1) * Q]
        out_ref[b, Q : 2 * Q, :] = side


def tile_of(recv_ref, t, lo):
    if t < BLOCKS:
        return recv_ref[t, lo : lo + 16, 0:128].astype(F32)
    p = 2 * (t - BLOCKS)
    return recv_ref[p, lo : lo + 16, 128:256].astype(F32) + recv_ref[p + 1, lo : lo + 16, 128:256].astype(F32)


def data_side(recv_ref, weight, onehot):
    sub = lax.broadcasted_iota(jnp.int32, (8, 128), 0) // KC
    row = (lax.broadcasted_iota(jnp.int32, (RK, 128), 0) // KC).astype(F32)
    for t in range(TILES):
        at = slice(t * 128, (t + 1) * 128)
        side = tile_of(recv_ref, t, Q)
        coef = 0.5 * (side[0:8] + pltpu.roll(side[0:8], KC, 0))
        rec, freq = side[8:9], side[9:10]
        for g in range(FK // 8):
            weight[g * 8 : g * 8 + 8, at] = jnp.where(freq == (sub + 2 * g).astype(F32), coef, 0.0)
        onehot[:, at] = jnp.where(rec == row, 1.0, 0.0).astype(BF)


def expand(weight, x_ref, basis, z, acc, v, n, width):
    acc[...] = jnp.zeros_like(acc)

    def step(i, _):
        at = pl.ds(pl.multiple_of(i * width, width), width)
        x = x_ref[:, at]
        for fk in range(FK):
            z[fk * Q : (fk + 1) * Q, :] = (weight[fk : fk + 1, at] * x).astype(BF)
        acc[...] += lax.dot_general(z[...], basis[:, at], NT, preferred_element_type=F32)
        return 0

    lax.fori_loop(0, n // width, step, 0)
    shape = (FK * Q, RK)
    k_row = lax.rem(lax.broadcasted_iota(jnp.int32, shape, 0) // Q, KC)
    k_col = lax.rem(lax.broadcasted_iota(jnp.int32, shape, 1), KC)
    v[...] = jnp.where(k_row == k_col, acc[...], 0.0).astype(BF)


def contract_tile(v, basis, weight):
    u = jnp.dot(v, basis, preferred_element_type=F32)
    total = [jnp.zeros((Q, u.shape[1]), F32) for _ in range(4)]
    for fk in range(FK):
        total[fk % 4] = total[fk % 4] + weight(fk) * u[fk * Q : (fk + 1) * Q, :]
    return (total[0] + total[1]) + (total[2] + total[3])


def smooth_rows(rows, first, last):
    lane = lax.broadcasted_iota(jnp.int32, (Q, COLS), 1)

    def sweep(rows):
        out = []
        for i in range(1, len(rows) - 1):
            x = rows[i]
            left = jnp.where(lane == 0, 0.0, pltpu.roll(x, 1, 1))
            right = jnp.where(lane == COLS - 1, 0.0, pltpu.roll(x, COLS - 1, 1))
            out.append(x + 0.2 * ((rows[i - 1] + rows[i + 1] + left + right) - 4.0 * x))
        return out

    once = sweep(rows)
    once[0] = once[0] * jnp.where(first, 0.0, 1.0)
    once[-1] = once[-1] * jnp.where(last, 0.0, 1.0)
    return sweep(once)


def cells_from_data(v, adj_ref, up_ref, down_ref, field, cell):
    def step(i, _):
        at = pl.ds(pl.multiple_of(i * 256, 256), 256)
        cell[:, at] = contract_tile(v[...], adj_ref[:, at], lambda fk: field[fk : fk + 1, at])
        return 0

    lax.fori_loop(0, CELLS // 256, step, 0)
    edges = []
    for i, edge in enumerate((up_ref, down_ref)):
        at = slice(CELLS + i * HALO, CELLS + (i + 1) * HALO)
        edges.append(contract_tile(v[...], edge[0:RK, :], lambda fk: field[fk : fk + 1, at]))
    up, down = edges
    rows = [up[:, 0:COLS], up[:, COLS:]]
    rows += [cell[:, r * COLS : (r + 1) * COLS] for r in range(GRID_ROWS)]
    rows += [down[:, 0:COLS], down[:, COLS:]]
    j = lax.axis_index("mp")
    return smooth_rows(rows, j == 0, j == SLABS - 1)


def load_fields(fwd_ref, up_ref, down_ref, field):
    field[:, 0:CELLS] = fwd_ref[...].astype(F32)
    field[:, CELLS : CELLS + HALO] = up_ref[RK:, :].astype(F32)
    field[:, CELLS + HALO :] = down_ref[RK:, :].astype(F32)


def gram_kernel(recv_ref, adj_ref, fwd_ref, up_ref, down_ref, gram_ref, tiles_ref, weight, onehot, field, x, cell, z, acc, v):
    load_fields(fwd_ref, up_ref, down_ref, field)
    data_side(recv_ref, weight, onehot)
    for t in range(TILES):
        tile = tile_of(recv_ref, t, 0)
        x[:, t * 128 : (t + 1) * 128] = tile
        tiles_ref[t] = tile
    for t in range(TILES, SLABS):
        tiles_ref[t] = jnp.zeros((Q, 128), F32)
        gram_ref[t] = jnp.zeros((Q, 128), F32)
    expand(weight, x, onehot, z, acc, v, NDATA, 512)
    rows = cells_from_data(v, adj_ref, up_ref, down_ref, field, cell)
    for r in range(GRID_ROWS):
        cell[:, r * COLS : (r + 1) * COLS] = rows[r] * (1.0 / (CELLS * SLABS))
    expand(field, cell, adj_ref, z, acc, v, CELLS, 512)

    def step(i, _):
        at = pl.ds(pl.multiple_of(i * 256, 256), 256)
        g = contract_tile(v[...], onehot[:, at], lambda fk: weight[fk : fk + 1, at])
        gram_ref[2 * i] = g[:, 0:128]
        gram_ref[2 * i + 1] = g[:, 128:256]
        return 0

    lax.fori_loop(0, TILES // 2, step, 0)


def update_kernel(parts_ref, tiles_ref, out_ref):
    total = tiles_ref[lax.axis_index("mp")]
    for j in range(SLABS):
        total = total + parts_ref[j]
    total = total.astype(BF)
    for j in range(SLABS):
        out_ref[j] = total


def model_kernel(recv_ref, upd_ref, adj_ref, fwd_ref, up_ref, down_ref, out_ref, weight, onehot, field, x, cell, z, acc, v):
    load_fields(fwd_ref, up_ref, down_ref, field)
    data_side(recv_ref, weight, onehot)
    for t in range(TILES):
        x[:, t * 128 : (t + 1) * 128] = upd_ref[t].astype(F32)
    expand(weight, x, onehot, z, acc, v, NDATA, 512)
    rows = cells_from_data(v, adj_ref, up_ref, down_ref, field, cell)
    for b in range(BLOCKS):
        out_ref[b, 0:Q, :] = (rows[b] * (1.0 / math.sqrt(NDATA))).astype(BF)
        out_ref[b, Q : 2 * Q, :] = upd_ref[b]
        out_ref[b, 2 * Q : 3 * Q, :] = upd_ref[BLOCKS + b // 2]


def finish_kernel(recv_ref, upd_ref, model_ref):
    odd = lax.rem(lax.axis_index("dp"), 2) == 1
    part = lambda i: jnp.concatenate([recv_ref[b, i * Q : (i + 1) * Q, :] for b in range(BLOCKS)], axis=0).astype(F32)
    model_ref[...] = jnp.transpose(part(0))
    upd_ref[0:128, :] = jnp.transpose(part(1)).astype(BF)
    tail = part(2)
    tail = jnp.where(odd, pltpu.roll(tail, 64, 1), tail)
    upd_ref[128:DATA, :] = jnp.transpose(tail)[0:64].astype(BF)


def per_device(forward_fields, adjoint_fields, data_rec, data_freq, data_coef, residual_cols):
    shape = jax.ShapeDtypeStruct
    params = pltpu.CompilerParams(vmem_limit_bytes=40 * 1024 * 1024)
    call = functools.partial(pl.pallas_call, compiler_params=params)
    adj = adjoint_fields.reshape(RK, CELLS)
    fwd = forward_fields.reshape(FK, CELLS)
    send_down = jnp.concatenate([adj[:, -HALO:], fwd[:, -HALO:]], axis=0)
    send_up = jnp.concatenate([adj[:, :HALO], fwd[:, :HALO]], axis=0)
    to_next = [(i, i + 1) for i in range(SLABS - 1)]
    up = lax.ppermute(send_down, "mp", to_next)
    down = lax.ppermute(send_up, "mp", [(b, a) for a, b in to_next])
    packed = call(
        pack_kernel,
        out_shape=shape((BLOCKS, 2 * Q, 256), BF),
        in_specs=whole(4),
        out_specs=whole(1)[0],
        scratch_shapes=[pltpu.VMEM((256, RHS), F32), pltpu.VMEM((256, 128), F32)],
    )(residual_cols, data_coef, data_rec.reshape(1, DATA), data_freq.reshape(1, DATA))
    recv = lax.all_to_all(packed, "dp", 0, 0)
    scratch = [
        pltpu.VMEM((FK, NDATA), F32),
        pltpu.VMEM((RK, NDATA), BF),
        pltpu.VMEM((FK, CELLS + 2 * HALO), F32),
        pltpu.VMEM((Q, NDATA), F32),
        pltpu.VMEM((Q, CELLS), F32),
        pltpu.VMEM((FK * Q, 512), BF),
        pltpu.VMEM((FK * Q, RK), F32),
        pltpu.VMEM((FK * Q, RK), BF),
    ]
    gram, tiles = call(
        gram_kernel,
        out_shape=[shape((SLABS, Q, 128), F32), shape((SLABS, Q, 128), F32)],
        in_specs=whole(5),
        out_specs=whole(2),
        scratch_shapes=scratch,
    )(recv, adj, fwd, up, down)
    parts = lax.all_to_all(gram, "mp", 0, 0)
    mine = call(update_kernel, out_shape=shape((SLABS, Q, 128), BF), in_specs=whole(2), out_specs=whole(1)[0])(parts, tiles)
    update = lax.all_to_all(mine, "mp", 0, 0)
    rows = call(
        model_kernel,
        out_shape=shape((BLOCKS, 3 * Q, 128), BF),
        in_specs=whole(6),
        out_specs=whole(1)[0],
        scratch_shapes=scratch,
    )(recv, update, adj, fwd, up, down)
    last = lax.all_to_all(rows, "dp", 0, 0)
    return call(
        finish_kernel,
        out_shape=[shape((DATA, RHS), BF), shape((COLS, RHS), F32)],
        in_specs=whole(1),
        out_specs=whole(2),
    )(last)


def solution(mesh):
    in_specs = (
        P(None, None, "mp"),
        P(None, None, "mp"),
        P("dp"),
        P("dp"),
        P("dp", None),
        P("dp", None),
    )
    out_specs = (P("dp", None), P(("mp", "dp"), None))
    return jax.shard_map(
        per_device, mesh=mesh, in_specs=in_specs, out_specs=out_specs, check_vma=False
    )
```

```python
import functools
import math

import jax
import jax.numpy as jnp
from jax import lax
from jax.experimental import pallas as pl
from jax.experimental.pallas import tpu as pltpu
from jax.sharding import PartitionSpec as P

BF, F32 = jnp.bfloat16, jnp.float32
COLS = 128
HALO = 2 * COLS
NREC, NFREQ, KC = 64, 16, 4
FK, RK = NFREQ * KC, NREC * KC
DATA, RHS, BLOCKS, SLABS = 192, 256, 16, 32
NDATA, CELLS = DATA * BLOCKS, 2048
Q = RHS // BLOCKS
TILES = NDATA // 128
GRID_ROWS = CELLS // COLS
NT = (((1,), (1,)), ((), ()))


NEAR = [
    [(j if i & 2 == 0 else j ^ 2) * BLOCKS + i for i in range(BLOCKS)] for j in range(SLABS)
]


def whole(n):
    return [pl.BlockSpec(memory_space=pltpu.VMEM)] * n


def pack_kernel(res_ref, coef_ref, rec_ref, freq_ref, out_ref, big, side):
    odd = lax.rem(lax.axis_index("dp"), 2) == 1
    big[...] = jnp.zeros_like(big)
    side[...] = jnp.zeros_like(side)
    big[0:DATA, :] = res_ref[...].astype(F32)
    coef = coef_ref[...]
    hi = coef.astype(BF).astype(F32)
    side[0:KC, 0:DATA] = hi
    side[KC : 2 * KC, 0:DATA] = coef - hi
    side[8:9, 0:DATA] = rec_ref[...].astype(F32)
    side[9:10, 0:DATA] = freq_ref[...].astype(F32)

    def place(v):
        tail = v[:, 128:256]
        tail = jnp.where(odd, pltpu.roll(tail, 64, 1), tail)
        return jnp.concatenate([v[:, 0:128], tail], axis=1).astype(BF)

    res = place(jnp.transpose(big[...]))
    rest = place(side[...])
    for b in range(BLOCKS):
        out_ref[b, 0:Q, :] = res[b * Q : (b + 1) * Q]
        out_ref[b, Q : 2 * Q, :] = rest


def tile_of(recv_ref, t, lo):
    if t < BLOCKS:
        return recv_ref[t, lo : lo + 16, 0:128].astype(F32)
    p = 2 * (t - BLOCKS)
    return recv_ref[p, lo : lo + 16, 128:256].astype(F32) + recv_ref[p + 1, lo : lo + 16, 128:256].astype(F32)


def pick_data(recv_ref, pick, freqs):
    sub = lax.broadcasted_iota(jnp.int32, (8, 128), 0) // KC
    for t in range(TILES):
        at = slice(t * 128, (t + 1) * 128)
        side = tile_of(recv_ref, t, Q)
        coef = 0.5 * (side[0:8] + pltpu.roll(side[0:8], KC, 0))
        rec = side[8:9]
        freqs[:, at] = jnp.broadcast_to(side[9:10], (8, 128))
        for g in range(RK // 16):
            two = [jnp.where(rec == (sub + 2 * (2 * g + i)).astype(F32), coef, 0.0) for i in range(2)]
            pick[g * 16 : g * 16 + 16, at] = jnp.concatenate(two, axis=0).astype(BF)


def of_component(v, k):
    lane = lax.rem(lax.broadcasted_iota(jnp.int32, v.shape, 1), KC)
    return jnp.where(lane == k, v, 0.0)


def from_data(tiles, pick, freqs, z, v):
    for t in range(TILES):
        at = slice(t * 128, (t + 1) * 128)
        x = tiles(t)
        freq = jnp.concatenate([freqs[:, at], freqs[:, at]], axis=0)
        for f in range(NFREQ):
            z[f * Q : (f + 1) * Q, at] = jnp.where(freq == float(f), x, 0.0).astype(BF)
    w = lax.dot_general(z[...], pick[...], NT, preferred_element_type=F32)
    for f in range(NFREQ):
        for k in range(KC):
            fk = f * KC + k
            v[fk * Q : (fk + 1) * Q, :] = of_component(w[f * Q : (f + 1) * Q], k).astype(BF)


def to_cells(v, basis, field):
    u = jnp.dot(v[...], basis, preferred_element_type=F32)
    total = [jnp.zeros((Q, u.shape[1]), F32) for _ in range(4)]
    for fk in range(FK):
        total[fk % 4] = total[fk % 4] + field(fk) * u[fk * Q : (fk + 1) * Q, :]
    return (total[0] + total[1]) + (total[2] + total[3])


def center_cells(v, adj_ref, field, cell):
    for i in range(CELLS // 256):
        at = slice(i * 256, (i + 1) * 256)
        cell[:, at] = to_cells(v, adj_ref[:, at], lambda fk: field[fk : fk + 1, at])


def with_edges(v, up_ref, down_ref, edge, cell):
    edge[:, 0:HALO] = up_ref[RK:, :].astype(F32)
    edge[:, HALO:] = down_ref[RK:, :].astype(F32)
    up = to_cells(v, up_ref[0:RK, :], lambda fk: edge[fk : fk + 1, 0:HALO])
    down = to_cells(v, down_ref[0:RK, :], lambda fk: edge[fk : fk + 1, HALO:])
    rows = [up[:, 0:COLS], up[:, COLS:]]
    rows += [cell[:, r * COLS : (r + 1) * COLS] for r in range(GRID_ROWS)]
    rows += [down[:, 0:COLS], down[:, COLS:]]
    j = lax.axis_index("mp")
    return smooth_rows(rows, j == 0, j == SLABS - 1)


def back_kernel(recv_ref, adj_ref, fwd_ref, pick, freqs, tiles_ref, v, field, cell, z):
    field[...] = fwd_ref[...].astype(F32)
    pick_data(recv_ref, pick, freqs)
    for t in range(TILES):
        tiles_ref[t] = tile_of(recv_ref, t, 0)
    for t in range(TILES, SLABS):
        tiles_ref[t] = jnp.zeros((Q, 128), F32)
    from_data(lambda t: tiles_ref[t], pick, freqs, z, v)
    center_cells(v, adj_ref, field, cell)


def gram_kernel(v, cell_ref, pick, freqs, field, adj_ref, up_ref, down_ref, gram_ref, edge, z, y):
    rows = with_edges(v, up_ref, down_ref, edge, cell_ref)
    for r in range(GRID_ROWS):
        at = slice(r * COLS, (r + 1) * COLS)
        x = rows[r] * (1.0 / (CELLS * SLABS))
        for fk in range(FK):
            z[fk * Q : (fk + 1) * Q, at] = (field[fk : fk + 1, at] * x).astype(BF)
    w = lax.dot_general(z[...], adj_ref[...], NT, preferred_element_type=F32)
    for f in range(NFREQ):
        part = [of_component(w[(f * KC + k) * Q : (f * KC + k + 1) * Q], k) for k in range(KC)]
        y[f * Q : (f + 1) * Q, :] = ((part[0] + part[1]) + (part[2] + part[3])).astype(BF)
    for i in range(TILES // 2):
        at = slice(i * 256, (i + 1) * 256)
        u = jnp.dot(y[...], pick[:, at], preferred_element_type=F32)
        freq = jnp.concatenate([freqs[:, at], freqs[:, at]], axis=0)
        g = jnp.zeros((Q, 256), F32)
        for f in range(NFREQ):
            g = jnp.where(freq == float(f), u[f * Q : (f + 1) * Q], g)
        gram_ref[2 * i] = g[:, 0:128]
        gram_ref[2 * i + 1] = g[:, 128:256]
    for t in range(TILES, SLABS):
        gram_ref[t] = jnp.zeros((Q, 128), F32)


def smooth_rows(rows, first, last):
    lane = lax.broadcasted_iota(jnp.int32, (Q, COLS), 1)

    def sweep(rows):
        out = []
        for i in range(1, len(rows) - 1):
            x = rows[i]
            left = jnp.where(lane == 0, 0.0, pltpu.roll(x, 1, 1))
            right = jnp.where(lane == COLS - 1, 0.0, pltpu.roll(x, COLS - 1, 1))
            out.append(x + 0.2 * ((rows[i - 1] + rows[i + 1] + left + right) - 4.0 * x))
        return out

    once = sweep(rows)
    once[0] = once[0] * jnp.where(first, 0.0, 1.0)
    once[-1] = once[-1] * jnp.where(last, 0.0, 1.0)
    return sweep(once)


def update_kernel(parts_ref, tiles_ref, out_ref):
    total = tiles_ref[lax.axis_index("mp")]
    for j in range(SLABS):
        total = total + parts_ref[j]
    total = total.astype(BF)
    for j in range(SLABS):
        out_ref[j] = total


def model_kernel(upd_ref, pick, freqs, field, adj_ref, up_ref, down_ref, out_ref, z, v, cell, edge):
    from_data(lambda t: upd_ref[t].astype(F32), pick, freqs, z, v)
    center_cells(v, adj_ref, field, cell)
    rows = with_edges(v, up_ref, down_ref, edge, cell)
    for b in range(BLOCKS):
        out_ref[b, 0:Q, :] = (rows[b] * (1.0 / math.sqrt(NDATA))).astype(BF)
        out_ref[b, Q : 2 * Q, :] = upd_ref[b]
        out_ref[b, 2 * Q : 3 * Q, :] = upd_ref[BLOCKS + b // 2]


def finish_kernel(recv_ref, upd_ref, model_ref):
    odd = lax.rem(lax.axis_index("dp"), 2) == 1
    part = lambda i: jnp.concatenate([recv_ref[b, i * Q : (i + 1) * Q, :] for b in range(BLOCKS)], axis=0).astype(F32)
    model_ref[...] = jnp.transpose(part(0))
    upd_ref[0:128, :] = jnp.transpose(part(1)).astype(BF)
    tail = part(2)
    tail = jnp.where(odd, pltpu.roll(tail, 64, 1), tail)
    upd_ref[128:DATA, :] = jnp.transpose(tail)[0:64].astype(BF)


def per_device(forward_fields, adjoint_fields, data_rec, data_freq, data_coef, residual_cols):
    shape = jax.ShapeDtypeStruct
    params = pltpu.CompilerParams(vmem_limit_bytes=40 * 1024 * 1024)
    call = functools.partial(pl.pallas_call, compiler_params=params)
    adj = adjoint_fields.reshape(RK, CELLS)
    fwd = forward_fields.reshape(FK, CELLS)
    send_down = jnp.concatenate([adj[:, -HALO:], fwd[:, -HALO:]], axis=0)
    send_up = jnp.concatenate([adj[:, :HALO], fwd[:, :HALO]], axis=0)
    to_next = [
        (j * BLOCKS + i, (j + 1) * BLOCKS + (i ^ 2 if j % 4 == 3 else i)) for j in range(SLABS - 1) for i in range(BLOCKS)
    ]
    up = lax.ppermute(send_down, ("mp", "dp"), to_next)
    down = lax.ppermute(send_up, ("mp", "dp"), [(b, a) for a, b in to_next])
    packed = call(
        pack_kernel,
        out_shape=shape((BLOCKS, 2 * Q, 256), BF),
        in_specs=whole(4),
        out_specs=whole(1)[0],
        scratch_shapes=[pltpu.VMEM((256, RHS), F32), pltpu.VMEM((2 * KC + 8, 256), F32)],
    )(residual_cols, data_coef.T, data_rec.reshape(1, DATA), data_freq.reshape(1, DATA))
    recv = lax.all_to_all(packed, ("mp", "dp"), 0, 0, axis_index_groups=NEAR)
    pick, freqs, tiles, v, field, cell = call(
        back_kernel,
        out_shape=[
            shape((RK, NDATA), BF),
            shape((8, NDATA), F32),
            shape((SLABS, Q, 128), F32),
            shape((FK * Q, RK), BF),
            shape((FK, CELLS), F32),
            shape((Q, CELLS), F32),
        ],
        in_specs=whole(3),
        out_specs=whole(6),
        scratch_shapes=[pltpu.VMEM((NFREQ * Q, NDATA), BF)],
        cost_estimate=pl.CostEstimate(flops=4 * 10**9, bytes_accessed=8 * 10**6, transcendentals=0),
    )(recv, adj, fwd)
    gram = call(
        gram_kernel,
        out_shape=shape((SLABS, Q, 128), F32),
        in_specs=whole(8),
        out_specs=whole(1)[0],
        scratch_shapes=[
            pltpu.VMEM((FK, 2 * HALO), F32),
            pltpu.VMEM((FK * Q, CELLS), BF),
            pltpu.VMEM((NFREQ * Q, RK), BF),
        ],
    )(v, cell, pick, freqs, field, adj, up, down)
    parts = lax.all_to_all(gram, "mp", 0, 0)
    mine = call(update_kernel, out_shape=shape((SLABS, Q, 128), BF), in_specs=whole(2), out_specs=whole(1)[0])(parts, tiles)
    update = lax.all_to_all(mine, "mp", 0, 0)
    rows = call(
        model_kernel,
        out_shape=shape((BLOCKS, 3 * Q, 128), BF),
        in_specs=whole(7),
        out_specs=whole(1)[0],
        scratch_shapes=[
            pltpu.VMEM((NFREQ * Q, NDATA), BF),
            pltpu.VMEM((FK * Q, RK), BF),
            pltpu.VMEM((Q, CELLS), F32),
            pltpu.VMEM((FK, 2 * HALO), F32),
        ],
    )(update, pick, freqs, field, adj, up, down)
    last = lax.all_to_all(rows, "dp", 0, 0)
    return call(
        finish_kernel,
        out_shape=[shape((DATA, RHS), BF), shape((COLS, RHS), F32)],
        in_specs=whole(1),
        out_specs=whole(2),
    )(last)


def solution(mesh):
    in_specs = (
        P(None, None, "mp"),
        P(None, None, "mp"),
        P("dp"),
        P("dp"),
        P("dp", None),
        P("dp", None),
    )
    out_specs = (P("dp", None), P(("mp", "dp"), None))
    return jax.shard_map(
        per_device, mesh=mesh, in_specs=in_specs, out_specs=out_specs, check_vma=False
    )
```

```python
import functools
import math

import jax
import jax.numpy as jnp
from jax import lax
from jax.experimental import pallas as pl
from jax.experimental.pallas import tpu as pltpu
from jax.sharding import PartitionSpec as P

BF, F32 = jnp.bfloat16, jnp.float32
COLS = 128
HALO = 2 * COLS
NREC, NFREQ, KC = 64, 16, 4
FK, RK = NFREQ * KC, NREC * KC
DATA, RHS, BLOCKS, SLABS = 192, 256, 16, 32
NDATA, CELLS = DATA * BLOCKS, 2048
Q = RHS // BLOCKS
TILES = NDATA // 128
GRID_ROWS = CELLS // COLS
NT = (((1,), (1,)), ((), ()))


NEAR = [
    [(j if i & 2 == 0 else j ^ 2) * BLOCKS + i for i in range(BLOCKS)] for j in range(SLABS)
]


def whole(n):
    return [pl.BlockSpec(memory_space=pltpu.VMEM)] * n


def pack_kernel(res_hbm, coef_hbm, rec_hbm, freq_hbm, out_ref, res_in, coef_in, rec_in, freq_in, sems, big, side):
    pairs = ((res_hbm, res_in), (coef_hbm, coef_in), (rec_hbm, rec_in), (freq_hbm, freq_in))
    copies = [pltpu.make_async_copy(src, dst, sems.at[i]) for i, (src, dst) in enumerate(pairs)]
    for copy in copies:
        copy.start()
    odd = lax.rem(lax.axis_index("dp"), 2) == 1
    big[DATA:, :] = jnp.zeros((256 - DATA, RHS), F32)
    side[...] = jnp.zeros_like(side)
    for copy in copies:
        copy.wait()
    big[0:DATA, :] = res_in[...].astype(F32)
    side[0:KC, 0:DATA] = coef_in[...]
    side[4:5, 0:DATA] = rec_in[...].astype(F32)
    side[5:6, 0:DATA] = freq_in[...].astype(F32)
    res = jnp.transpose(big[...])
    head, tail = side[:, 0:128], pltpu.roll(side[:, 128:256], 64, 1)
    for b in range(BLOCKS):
        mine = res[b * Q : (b + 1) * Q]
        more = mine[:, 128:256]
        more = jnp.concatenate([more[0:8] + tail, more[8:16]], axis=0)
        more = jnp.where(odd, pltpu.roll(more, 64, 1), more)
        out_ref[b] = jnp.concatenate([mine[:, 0:128], more, head], axis=0).astype(BF)


def unpack(recv_ref, tiles_ref, side):
    low = lax.broadcasted_iota(jnp.int32, (Q, 128), 1) < 64
    for p in range(BLOCKS // 2):
        even, odd = recv_ref[2 * p].astype(F32), recv_ref[2 * p + 1].astype(F32)
        for i, piece in enumerate((even, odd)):
            t = 2 * p + i
            tiles_ref[t] = piece[0:Q]
            side[:, t * 128 : (t + 1) * 128] = piece[2 * Q :]
        t = BLOCKS + p
        even, odd = even[Q : 2 * Q], odd[Q : 2 * Q]
        tiles_ref[t] = jnp.where(low, even, odd)
        side[:, t * 128 : (t + 1) * 128] = pltpu.roll(jnp.where(low[0:8], odd[0:8], even[0:8]), 64, 1)
    for t in range(TILES, SLABS):
        tiles_ref[t] = jnp.zeros((Q, 128), F32)


def pick_data(side, pick, freqs):
    row = lax.broadcasted_iota(jnp.int32, (8, 128), 0)
    recs = [(row // KC + 2 * g).astype(F32) for g in range(RK // 8)]
    for t in range(TILES):
        at = slice(t * 128, (t + 1) * 128)
        v = side[:, at]
        coef = 0.5 * jnp.where(row < KC, v, pltpu.roll(v, KC, 0))
        rec = jnp.broadcast_to(v[4:5], (8, 128))
        freqs[:, at] = jnp.broadcast_to(v[5:6], (8, 128))
        for g in range(RK // 16):
            two = [jnp.where(rec == recs[2 * g + i], coef, 0.0) for i in range(2)]
            pick[g * 16 : g * 16 + 16, at] = jnp.concatenate(two, axis=0).astype(BF)


def of_component(v, k):
    lane = lax.rem(lax.broadcasted_iota(jnp.int32, v.shape, 1), KC)
    return jnp.where(lane == k, v, 0.0)


def from_data(tiles, pick, freqs, z, v):
    for t in range(TILES):
        at = slice(t * 128, (t + 1) * 128)
        x = tiles(t)
        freq = jnp.concatenate([freqs[:, at], freqs[:, at]], axis=0)
        for f in range(NFREQ):
            z[f * Q : (f + 1) * Q, at] = jnp.where(freq == float(f), x, 0.0).astype(BF)
    w = lax.dot_general(z[...], pick[...], NT, preferred_element_type=F32)
    for f in range(NFREQ):
        for k in range(KC):
            fk = f * KC + k
            v[fk * Q : (fk + 1) * Q, :] = of_component(w[f * Q : (f + 1) * Q], k).astype(BF)


def to_cells(v, basis, field):
    u = jnp.dot(v[...], basis, preferred_element_type=F32)
    total = [jnp.zeros((Q, u.shape[1]), F32) for _ in range(4)]
    for fk in range(FK):
        total[fk % 4] = total[fk % 4] + field(fk) * u[fk * Q : (fk + 1) * Q, :]
    return (total[0] + total[1]) + (total[2] + total[3])


def center_cells(v, adj_ref, field, cell):
    for i in range(CELLS // 256):
        at = slice(i * 256, (i + 1) * 256)
        cell[:, at] = to_cells(v, adj_ref[:, at], lambda fk: field[fk : fk + 1, at])


def with_edges(v, up_ref, down_ref, edge, cell):
    edge[:, 0:HALO] = up_ref[RK:, :].astype(F32)
    edge[:, HALO:] = down_ref[RK:, :].astype(F32)
    up = to_cells(v, up_ref[0:RK, :], lambda fk: edge[fk : fk + 1, 0:HALO])
    down = to_cells(v, down_ref[0:RK, :], lambda fk: edge[fk : fk + 1, HALO:])
    rows = [up[:, 0:COLS], up[:, COLS:]]
    rows += [cell[:, r * COLS : (r + 1) * COLS] for r in range(GRID_ROWS)]
    rows += [down[:, 0:COLS], down[:, COLS:]]
    j = lax.axis_index("mp")
    return smooth_rows(rows, j == 0, j == SLABS - 1)


def back_kernel(recv_ref, adj_ref, fwd_ref, pick, freqs, tiles_ref, v, field, cell, z, side):
    unpack(recv_ref, tiles_ref, side)
    pick_data(side, pick, freqs)
    field[...] = fwd_ref[...].astype(F32)
    from_data(lambda t: tiles_ref[t], pick, freqs, z, v)
    center_cells(v, adj_ref, field, cell)


def gram_kernel(v, cell_ref, pick, freqs, field, adj_ref, up_ref, down_ref, gram_ref, edge, z, y):
    rows = with_edges(v, up_ref, down_ref, edge, cell_ref)
    for r in range(GRID_ROWS):
        at = slice(r * COLS, (r + 1) * COLS)
        x = rows[r] * (1.0 / (CELLS * SLABS))
        for fk in range(FK):
            z[fk * Q : (fk + 1) * Q, at] = (field[fk : fk + 1, at] * x).astype(BF)
    w = lax.dot_general(z[...], adj_ref[...], NT, preferred_element_type=F32)
    for f in range(NFREQ):
        part = [of_component(w[(f * KC + k) * Q : (f * KC + k + 1) * Q], k) for k in range(KC)]
        y[f * Q : (f + 1) * Q, :] = ((part[0] + part[1]) + (part[2] + part[3])).astype(BF)
    for i in range(TILES // 2):
        at = slice(i * 256, (i + 1) * 256)
        u = jnp.dot(y[...], pick[:, at], preferred_element_type=F32)
        freq = jnp.concatenate([freqs[:, at], freqs[:, at]], axis=0)
        g = jnp.zeros((Q, 256), F32)
        for f in range(NFREQ):
            g = jnp.where(freq == float(f), u[f * Q : (f + 1) * Q], g)
        gram_ref[2 * i] = g[:, 0:128]
        gram_ref[2 * i + 1] = g[:, 128:256]
    for t in range(TILES, SLABS):
        gram_ref[t] = jnp.zeros((Q, 128), F32)


def smooth_rows(rows, first, last):
    lane = lax.broadcasted_iota(jnp.int32, (Q, COLS), 1)

    def sweep(rows):
        out = []
        for i in range(1, len(rows) - 1):
            x = rows[i]
            left = jnp.where(lane == 0, 0.0, pltpu.roll(x, 1, 1))
            right = jnp.where(lane == COLS - 1, 0.0, pltpu.roll(x, COLS - 1, 1))
            out.append(x + 0.2 * ((rows[i - 1] + rows[i + 1] + left + right) - 4.0 * x))
        return out

    once = sweep(rows)
    once[0] = once[0] * jnp.where(first, 0.0, 1.0)
    once[-1] = once[-1] * jnp.where(last, 0.0, 1.0)
    return sweep(once)


def update_kernel(parts_ref, tiles_ref, out_ref):
    total = tiles_ref[lax.axis_index("mp")]
    for j in range(SLABS):
        total = total + parts_ref[j]
    total = total.astype(BF)
    for j in range(SLABS):
        out_ref[j] = total


def model_kernel(upd_ref, pick, freqs, field, adj_ref, up_ref, down_ref, out_ref, z, v, cell, edge):
    from_data(lambda t: upd_ref[t].astype(F32), pick, freqs, z, v)
    center_cells(v, adj_ref, field, cell)
    rows = with_edges(v, up_ref, down_ref, edge, cell)
    low = lax.broadcasted_iota(jnp.int32, (8, 128), 1) < 64
    for b in range(BLOCKS):
        tail = upd_ref[BLOCKS + b // 2].astype(F32)
        turned = pltpu.roll(tail, 64, 1)
        tail = jnp.where(low, tail[0:8], turned[8:16]) if b % 2 == 0 else jnp.where(low, turned[0:8], tail[8:16])
        piece = [rows[b] * (1.0 / math.sqrt(NDATA)), upd_ref[b].astype(F32), tail]
        out_ref[b] = jnp.concatenate(piece, axis=0).astype(BF)


def finish_kernel(recv_ref, upd_ref, model_ref):
    pieces = [recv_ref[b].astype(F32) for b in range(BLOCKS)]
    model_ref[...] = jnp.transpose(jnp.concatenate([p[0:Q] for p in pieces], axis=0))
    upd_ref[0:128, :] = jnp.transpose(jnp.concatenate([p[Q : 2 * Q] for p in pieces], axis=0)).astype(BF)
    tail = []
    for p in pieces:
        tail += [p[2 * Q :], pltpu.roll(p[2 * Q :], 64, 1)]
    upd_ref[128:DATA, :] = jnp.transpose(jnp.concatenate(tail, axis=0))[0:64].astype(BF)


def per_device(forward_fields, adjoint_fields, data_rec, data_freq, data_coef, residual_cols):
    shape = jax.ShapeDtypeStruct
    params = pltpu.CompilerParams(vmem_limit_bytes=40 * 1024 * 1024)
    call = functools.partial(pl.pallas_call, compiler_params=params)
    adj = adjoint_fields.reshape(RK, CELLS)
    fwd = forward_fields.reshape(FK, CELLS)
    send_down = jnp.concatenate([adj[:, -HALO:], fwd[:, -HALO:]], axis=0)
    send_up = jnp.concatenate([adj[:, :HALO], fwd[:, :HALO]], axis=0)
    to_next = [
        (j * BLOCKS + i, (j + 1) * BLOCKS + (i ^ 2 if j % 4 == 3 else i)) for j in range(SLABS - 1) for i in range(BLOCKS)
    ]
    up = lax.ppermute(send_down, ("mp", "dp"), to_next)
    down = lax.ppermute(send_up, ("mp", "dp"), [(b, a) for a, b in to_next])
    packed = pl.pallas_call(
        pack_kernel,
        compiler_params=pltpu.CompilerParams(vmem_limit_bytes=60 * 1024 * 1024),
        out_shape=shape((BLOCKS, 2 * Q + 8, 128), BF),
        in_specs=[pl.BlockSpec(memory_space=pl.ANY)] * 4,
        out_specs=whole(1)[0],
        scratch_shapes=[
            pltpu.VMEM((DATA, RHS), BF),
            pltpu.VMEM((KC, DATA), F32),
            pltpu.VMEM((1, DATA), jnp.int32),
            pltpu.VMEM((1, DATA), jnp.int32),
            pltpu.SemaphoreType.DMA((4,)),
            pltpu.VMEM((256, RHS), F32),
            pltpu.VMEM((8, 256), F32),
        ],
    )(residual_cols, data_coef.T, data_rec.reshape(1, DATA), data_freq.reshape(1, DATA))
    recv = lax.all_to_all(packed, ("mp", "dp"), 0, 0, axis_index_groups=NEAR)
    pick, freqs, tiles, v, field, cell = call(
        back_kernel,
        out_shape=[
            shape((RK, NDATA), BF),
            shape((8, NDATA), F32),
            shape((SLABS, Q, 128), F32),
            shape((FK * Q, RK), BF),
            shape((FK, CELLS), F32),
            shape((Q, CELLS), F32),
        ],
        in_specs=whole(3),
        out_specs=whole(6),
        scratch_shapes=[pltpu.VMEM((NFREQ * Q, NDATA), BF), pltpu.VMEM((8, NDATA), F32)],
        cost_estimate=pl.CostEstimate(flops=4 * 10**9, bytes_accessed=8 * 10**6, transcendentals=0),
    )(recv, adj, fwd)
    gram = call(
        gram_kernel,
        out_shape=shape((SLABS, Q, 128), F32),
        in_specs=whole(8),
        out_specs=whole(1)[0],
        scratch_shapes=[
            pltpu.VMEM((FK, 2 * HALO), F32),
            pltpu.VMEM((FK * Q, CELLS), BF),
            pltpu.VMEM((NFREQ * Q, RK), BF),
        ],
    )(v, cell, pick, freqs, field, adj, up, down)
    parts = lax.all_to_all(gram, "mp", 0, 0)
    mine = call(update_kernel, out_shape=shape((SLABS, Q, 128), BF), in_specs=whole(2), out_specs=whole(1)[0])(parts, tiles)
    update = lax.all_to_all(mine, "mp", 0, 0)
    rows = call(
        model_kernel,
        out_shape=shape((BLOCKS, 2 * Q + 8, 128), BF),
        in_specs=whole(7),
        out_specs=whole(1)[0],
        scratch_shapes=[
            pltpu.VMEM((NFREQ * Q, NDATA), BF),
            pltpu.VMEM((FK * Q, RK), BF),
            pltpu.VMEM((Q, CELLS), F32),
            pltpu.VMEM((FK, 2 * HALO), F32),
        ],
    )(update, pick, freqs, field, adj, up, down)
    last = lax.all_to_all(rows, "dp", 0, 0)
    return call(
        finish_kernel,
        out_shape=[shape((DATA, RHS), BF), shape((COLS, RHS), F32)],
        in_specs=whole(1),
        out_specs=whole(2),
    )(last)


def solution(mesh):
    in_specs = (
        P(None, None, "mp"),
        P(None, None, "mp"),
        P("dp"),
        P("dp"),
        P("dp", None),
        P("dp", None),
    )
    out_specs = (P("dp", None), P(("mp", "dp"), None))
    return jax.shard_map(
        per_device, mesh=mesh, in_specs=in_specs, out_specs=out_specs, check_vma=False
    )
```

```python
import functools
import math

import jax
import jax.numpy as jnp
from jax import lax
from jax.experimental import pallas as pl
from jax.experimental.pallas import tpu as pltpu
from jax.sharding import PartitionSpec as P

BF, F32 = jnp.bfloat16, jnp.float32
COLS = 128
HALO = 2 * COLS
NREC, NFREQ, KC = 64, 16, 4
FK, RK = NFREQ * KC, NREC * KC
DATA, RHS, BLOCKS, SLABS = 192, 256, 16, 32
NDATA, CELLS = DATA * BLOCKS, 2048
Q = RHS // BLOCKS
TILES = NDATA // 128
GRID_ROWS = CELLS // COLS
NT = (((1,), (1,)), ((), ()))


NEAR = [
    [(j if i & 2 == 0 else j ^ 2) * BLOCKS + i for i in range(BLOCKS)] for j in range(SLABS)
]


ALONG_Z = [[z * 4 + y for z in range(8)] for y in range(4)]


def whole(n):
    return [pl.BlockSpec(memory_space=pltpu.VMEM)] * n


def pack_kernel(res_hbm, coef_hbm, rec_hbm, freq_hbm, out_ref, res_in, coef_in, rec_in, freq_in, sems, big, side):
    pairs = ((res_hbm, res_in), (coef_hbm, coef_in), (rec_hbm, rec_in), (freq_hbm, freq_in))
    copies = [pltpu.make_async_copy(src, dst, sems.at[i]) for i, (src, dst) in enumerate(pairs)]
    for copy in copies:
        copy.start()
    odd = lax.rem(lax.axis_index("dp"), 2) == 1
    big[DATA:, :] = jnp.zeros((256 - DATA, RHS), F32)
    side[...] = jnp.zeros_like(side)
    for copy in copies:
        copy.wait()
    big[0:DATA, :] = res_in[...].astype(F32)
    side[0:KC, 0:DATA] = coef_in[...]
    side[4:5, 0:DATA] = rec_in[...].astype(F32)
    side[5:6, 0:DATA] = freq_in[...].astype(F32)
    res = jnp.transpose(big[...])
    head, tail = side[:, 0:128], pltpu.roll(side[:, 128:256], 64, 1)
    for b in range(BLOCKS):
        mine = res[b * Q : (b + 1) * Q]
        more = mine[:, 128:256]
        more = jnp.concatenate([more[0:8] + tail, more[8:16]], axis=0)
        more = jnp.where(odd, pltpu.roll(more, 64, 1), more)
        out_ref[b] = jnp.concatenate([mine[:, 0:128], more, head], axis=0).astype(BF)


def unpack(recv_ref, tiles_ref, side):
    low = lax.broadcasted_iota(jnp.int32, (Q, 128), 1) < 64
    for p in range(BLOCKS // 2):
        even, odd = recv_ref[2 * p].astype(F32), recv_ref[2 * p + 1].astype(F32)
        for i, piece in enumerate((even, odd)):
            t = 2 * p + i
            tiles_ref[t] = piece[0:Q]
            side[:, t * 128 : (t + 1) * 128] = piece[2 * Q :]
        t = BLOCKS + p
        even, odd = even[Q : 2 * Q], odd[Q : 2 * Q]
        tiles_ref[t] = jnp.where(low, even, odd)
        side[:, t * 128 : (t + 1) * 128] = pltpu.roll(jnp.where(low[0:8], odd[0:8], even[0:8]), 64, 1)
    for t in range(TILES, SLABS):
        tiles_ref[t] = jnp.zeros((Q, 128), F32)


def pick_data(side, pick, freqs):
    row = lax.broadcasted_iota(jnp.int32, (8, 128), 0)
    recs = [(row // KC + 2 * g).astype(F32) for g in range(RK // 8)]
    for t in range(TILES):
        at = slice(t * 128, (t + 1) * 128)
        v = side[:, at]
        coef = 0.5 * jnp.where(row < KC, v, pltpu.roll(v, KC, 0))
        rec = jnp.broadcast_to(v[4:5], (8, 128))
        freqs[:, at] = jnp.broadcast_to(v[5:6], (8, 128))
        for g in range(RK // 16):
            two = [jnp.where(rec == recs[2 * g + i], coef, 0.0) for i in range(2)]
            pick[g * 16 : g * 16 + 16, at] = jnp.concatenate(two, axis=0).astype(BF)


def of_component(v, k):
    lane = lax.rem(lax.broadcasted_iota(jnp.int32, v.shape, 1), KC)
    return jnp.where(lane == k, v, 0.0)


def from_data(tiles, pick, freqs, z, v):
    for t in range(TILES):
        at = slice(t * 128, (t + 1) * 128)
        x = tiles(t)
        freq = jnp.concatenate([freqs[:, at], freqs[:, at]], axis=0)
        for f in range(NFREQ):
            z[f * Q : (f + 1) * Q, at] = jnp.where(freq == float(f), x, 0.0).astype(BF)
    w = lax.dot_general(z[...], pick[...], NT, preferred_element_type=F32)
    for f in range(NFREQ):
        for k in range(KC):
            fk = f * KC + k
            v[fk * Q : (fk + 1) * Q, :] = of_component(w[f * Q : (f + 1) * Q], k).astype(BF)


def to_cells(v, basis, field):
    u = jnp.dot(v[...], basis, preferred_element_type=F32)
    total = [jnp.zeros((Q, u.shape[1]), F32) for _ in range(4)]
    for fk in range(FK):
        total[fk % 4] = total[fk % 4] + field(fk) * u[fk * Q : (fk + 1) * Q, :]
    return (total[0] + total[1]) + (total[2] + total[3])


def center_cells(v, adj_ref, field, cell):
    for i in range(CELLS // 256):
        at = slice(i * 256, (i + 1) * 256)
        cell[:, at] = to_cells(v, adj_ref[:, at], lambda fk: field[fk : fk + 1, at])


def with_edges(v, up_ref, down_ref, edge, cell):
    edge[:, 0:HALO] = up_ref[RK:, :].astype(F32)
    edge[:, HALO:] = down_ref[RK:, :].astype(F32)
    up = to_cells(v, up_ref[0:RK, :], lambda fk: edge[fk : fk + 1, 0:HALO])
    down = to_cells(v, down_ref[0:RK, :], lambda fk: edge[fk : fk + 1, HALO:])
    rows = [up[:, 0:COLS], up[:, COLS:]]
    rows += [cell[:, r * COLS : (r + 1) * COLS] for r in range(GRID_ROWS)]
    rows += [down[:, 0:COLS], down[:, COLS:]]
    j = lax.axis_index("mp")
    return smooth_rows(rows, j == 0, j == SLABS - 1)


def back_kernel(recv_ref, adj_ref, fwd_ref, pick, freqs, tiles_ref, v, field, cell, z, side):
    unpack(recv_ref, tiles_ref, side)
    pick_data(side, pick, freqs)
    field[...] = fwd_ref[...].astype(F32)
    from_data(lambda t: tiles_ref[t], pick, freqs, z, v)
    center_cells(v, adj_ref, field, cell)


def gram_kernel(v, cell_ref, pick, freqs, field, adj_ref, up_ref, down_ref, gram_ref, edge, z, y):
    rows = with_edges(v, up_ref, down_ref, edge, cell_ref)
    for r in range(GRID_ROWS):
        at = slice(r * COLS, (r + 1) * COLS)
        x = rows[r] * (1.0 / (CELLS * SLABS))
        for fk in range(FK):
            z[fk * Q : (fk + 1) * Q, at] = (field[fk : fk + 1, at] * x).astype(BF)
    w = lax.dot_general(z[...], adj_ref[...], NT, preferred_element_type=F32)
    for f in range(NFREQ):
        part = [of_component(w[(f * KC + k) * Q : (f * KC + k + 1) * Q], k) for k in range(KC)]
        y[f * Q : (f + 1) * Q, :] = ((part[0] + part[1]) + (part[2] + part[3])).astype(BF)
    for i in range(TILES // 2):
        at = slice(i * 256, (i + 1) * 256)
        u = jnp.dot(y[...], pick[:, at], preferred_element_type=F32)
        freq = jnp.concatenate([freqs[:, at], freqs[:, at]], axis=0)
        g = jnp.zeros((Q, 256), F32)
        for f in range(NFREQ):
            g = jnp.where(freq == float(f), u[f * Q : (f + 1) * Q], g)
        gram_ref[2 * i] = g[:, 0:128].astype(BF)
        gram_ref[2 * i + 1] = g[:, 128:256].astype(BF)


def smooth_rows(rows, first, last):
    lane = lax.broadcasted_iota(jnp.int32, (Q, COLS), 1)

    def sweep(rows):
        out = []
        for i in range(1, len(rows) - 1):
            x = rows[i]
            left = jnp.where(lane == 0, 0.0, pltpu.roll(x, 1, 1))
            right = jnp.where(lane == COLS - 1, 0.0, pltpu.roll(x, COLS - 1, 1))
            out.append(x + 0.2 * ((rows[i - 1] + rows[i + 1] + left + right) - 4.0 * x))
        return out

    once = sweep(rows)
    once[0] = once[0] * jnp.where(first, 0.0, 1.0)
    once[-1] = once[-1] * jnp.where(last, 0.0, 1.0)
    return sweep(once)


def update_kernel(parts_ref, out_ref):
    total = parts_ref[0].astype(F32)
    for z in range(1, 8):
        total = total + parts_ref[z].astype(F32)
    total = total.astype(BF)
    for j in range(SLABS):
        out_ref[j] = total


def model_kernel(sums_ref, tiles_ref, pick, freqs, field, adj_ref, up_ref, down_ref, out_ref, z, v, cell, edge, upd_ref):
    for t in range(TILES):
        at = slice((t % 3) * Q, (t % 3 + 1) * Q)
        part = [sums_ref[(t // 3) * 4 + y, at, :].astype(F32) for y in range(4)]
        upd_ref[t] = (((part[0] + part[1]) + (part[2] + part[3])) + tiles_ref[t]).astype(BF).astype(F32)
    from_data(lambda t: upd_ref[t], pick, freqs, z, v)
    center_cells(v, adj_ref, field, cell)
    rows = with_edges(v, up_ref, down_ref, edge, cell)
    low = lax.broadcasted_iota(jnp.int32, (8, 128), 1) < 64
    for b in range(BLOCKS):
        tail = upd_ref[BLOCKS + b // 2]
        turned = pltpu.roll(tail, 64, 1)
        tail = jnp.where(low, tail[0:8], turned[8:16]) if b % 2 == 0 else jnp.where(low, turned[0:8], tail[8:16])
        piece = [rows[b] * (1.0 / math.sqrt(NDATA)), upd_ref[b], tail]
        out_ref[b] = jnp.concatenate(piece, axis=0).astype(BF)


def finish_kernel(recv_ref, upd_ref, model_ref):
    pieces = [recv_ref[b].astype(F32) for b in range(BLOCKS)]
    model_ref[...] = jnp.transpose(jnp.concatenate([p[0:Q] for p in pieces], axis=0))
    upd_ref[0:128, :] = jnp.transpose(jnp.concatenate([p[Q : 2 * Q] for p in pieces], axis=0)).astype(BF)
    tail = []
    for p in pieces:
        tail += [p[2 * Q :], pltpu.roll(p[2 * Q :], 64, 1)]
    upd_ref[128:DATA, :] = jnp.transpose(jnp.concatenate(tail, axis=0))[0:64].astype(BF)


def per_device(forward_fields, adjoint_fields, data_rec, data_freq, data_coef, residual_cols):
    shape = jax.ShapeDtypeStruct
    params = pltpu.CompilerParams(vmem_limit_bytes=40 * 1024 * 1024)
    call = functools.partial(pl.pallas_call, compiler_params=params)
    adj = adjoint_fields.reshape(RK, CELLS)
    fwd = forward_fields.reshape(FK, CELLS)
    send_down = jnp.concatenate([adj[:, -HALO:], fwd[:, -HALO:]], axis=0)
    send_up = jnp.concatenate([adj[:, :HALO], fwd[:, :HALO]], axis=0)
    to_next = [
        (j * BLOCKS + i, (j + 1) * BLOCKS + (i ^ 2 if j % 4 == 3 else i)) for j in range(SLABS - 1) for i in range(BLOCKS)
    ]
    up = lax.ppermute(send_down, ("mp", "dp"), to_next)
    down = lax.ppermute(send_up, ("mp", "dp"), [(b, a) for a, b in to_next])
    packed = pl.pallas_call(
        pack_kernel,
        compiler_params=pltpu.CompilerParams(vmem_limit_bytes=60 * 1024 * 1024),
        out_shape=shape((BLOCKS, 2 * Q + 8, 128), BF),
        in_specs=[pl.BlockSpec(memory_space=pl.ANY)] * 4,
        out_specs=whole(1)[0],
        scratch_shapes=[
            pltpu.VMEM((DATA, RHS), BF),
            pltpu.VMEM((KC, DATA), F32),
            pltpu.VMEM((1, DATA), jnp.int32),
            pltpu.VMEM((1, DATA), jnp.int32),
            pltpu.SemaphoreType.DMA((4,)),
            pltpu.VMEM((256, RHS), F32),
            pltpu.VMEM((8, 256), F32),
        ],
    )(residual_cols, data_coef.T, data_rec.reshape(1, DATA), data_freq.reshape(1, DATA))
    recv = lax.all_to_all(packed, ("mp", "dp"), 0, 0, axis_index_groups=NEAR)
    pick, freqs, tiles, v, field, cell = call(
        back_kernel,
        out_shape=[
            shape((RK, NDATA), BF),
            shape((8, NDATA), F32),
            shape((SLABS, Q, 128), F32),
            shape((FK * Q, RK), BF),
            shape((FK, CELLS), F32),
            shape((Q, CELLS), F32),
        ],
        in_specs=whole(3),
        out_specs=whole(6),
        scratch_shapes=[pltpu.VMEM((NFREQ * Q, NDATA), BF), pltpu.VMEM((8, NDATA), F32)],
        cost_estimate=pl.CostEstimate(flops=4 * 10**9, bytes_accessed=8 * 10**6, transcendentals=0),
    )(recv, adj, fwd)
    gram = call(
        gram_kernel,
        out_shape=shape((TILES, Q, 128), BF),
        in_specs=whole(8),
        out_specs=whole(1)[0],
        scratch_shapes=[
            pltpu.VMEM((FK, 2 * HALO), F32),
            pltpu.VMEM((FK * Q, CELLS), BF),
            pltpu.VMEM((NFREQ * Q, RK), BF),
        ],
    )(v, cell, pick, freqs, field, adj, up, down)
    parts = lax.all_to_all(gram.reshape(8, 3 * Q, 128), "mp", 0, 0, axis_index_groups=ALONG_Z)
    mine = call(update_kernel, out_shape=shape((SLABS, 3 * Q, 128), BF), in_specs=whole(1), out_specs=whole(1)[0])(parts)
    update = lax.all_to_all(mine, "mp", 0, 0)
    rows = call(
        model_kernel,
        out_shape=shape((BLOCKS, 2 * Q + 8, 128), BF),
        in_specs=whole(8),
        out_specs=whole(1)[0],
        scratch_shapes=[
            pltpu.VMEM((NFREQ * Q, NDATA), BF),
            pltpu.VMEM((FK * Q, RK), BF),
            pltpu.VMEM((Q, CELLS), F32),
            pltpu.VMEM((FK, 2 * HALO), F32),
            pltpu.VMEM((TILES, Q, 128), F32),
        ],
    )(update, tiles, pick, freqs, field, adj, up, down)
    last = lax.all_to_all(rows, "dp", 0, 0)
    return call(
        finish_kernel,
        out_shape=[shape((DATA, RHS), BF), shape((COLS, RHS), F32)],
        in_specs=whole(1),
        out_specs=whole(2),
    )(last)


def solution(mesh):
    in_specs = (
        P(None, None, "mp"),
        P(None, None, "mp"),
        P("dp"),
        P("dp"),
        P("dp", None),
        P("dp", None),
    )
    out_specs = (P("dp", None), P(("mp", "dp"), None))
    return jax.shard_map(
        per_device, mesh=mesh, in_specs=in_specs, out_specs=out_specs, check_vma=False
    )
```

```python
import functools
import math

import jax
import jax.numpy as jnp
from jax import lax
from jax.experimental import pallas as pl
from jax.experimental.pallas import tpu as pltpu
from jax.sharding import PartitionSpec as P

BF, F32 = jnp.bfloat16, jnp.float32
COLS = 128
HALO = 2 * COLS
NREC, NFREQ, KC = 64, 16, 4
FK, RK = NFREQ * KC, NREC * KC
DATA, RHS, BLOCKS, SLABS = 192, 256, 16, 32
NDATA, CELLS = DATA * BLOCKS, 2048
Q = RHS // BLOCKS
TILES = NDATA // 128
GRID_ROWS = CELLS // COLS
NT = (((1,), (1,)), ((), ()))


NEAR = [
    [(j if i & 2 == 0 else j ^ 2) * BLOCKS + i for i in range(BLOCKS)] for j in range(SLABS)
]


ALONG_Z = [[z * 4 + y for z in range(8)] for y in range(4)]


def whole(n):
    return [pl.BlockSpec(memory_space=pltpu.VMEM)] * n


def pack_kernel(res_hbm, coef_hbm, rec_hbm, freq_hbm, out_ref, res_in, coef_in, rec_in, freq_in, sems, big, side):
    pairs = ((res_hbm, res_in), (coef_hbm, coef_in), (rec_hbm, rec_in), (freq_hbm, freq_in))
    copies = [pltpu.make_async_copy(src, dst, sems.at[i]) for i, (src, dst) in enumerate(pairs)]
    for copy in copies:
        copy.start()
    odd = lax.rem(lax.axis_index("dp"), 2) == 1
    big[DATA:, :] = jnp.zeros((256 - DATA, RHS), F32)
    side[...] = jnp.zeros_like(side)
    for copy in copies:
        copy.wait()
    big[0:DATA, :] = res_in[...].astype(F32)
    side[0:KC, 0:DATA] = coef_in[...]
    side[4:5, 0:DATA] = rec_in[...].astype(F32)
    side[5:6, 0:DATA] = freq_in[...].astype(F32)
    res = jnp.transpose(big[...])
    head, tail = side[:, 0:128], pltpu.roll(side[:, 128:256], 64, 1)
    for b in range(BLOCKS):
        mine = res[b * Q : (b + 1) * Q]
        more = mine[:, 128:256]
        more = jnp.concatenate([more[0:8] + tail, more[8:16]], axis=0)
        more = jnp.where(odd, pltpu.roll(more, 64, 1), more)
        out_ref[b] = jnp.concatenate([mine[:, 0:128], more, head], axis=0).astype(BF)


def unpack(recv_ref, tiles_ref, side):
    low = lax.broadcasted_iota(jnp.int32, (Q, 128), 1) < 64
    for p in range(BLOCKS // 2):
        even, odd = recv_ref[2 * p].astype(F32), recv_ref[2 * p + 1].astype(F32)
        for i, piece in enumerate((even, odd)):
            t = 2 * p + i
            tiles_ref[t] = piece[0:Q]
            side[:, t * 128 : (t + 1) * 128] = piece[2 * Q :]
        t = BLOCKS + p
        even, odd = even[Q : 2 * Q], odd[Q : 2 * Q]
        tiles_ref[t] = jnp.where(low, even, odd)
        side[:, t * 128 : (t + 1) * 128] = pltpu.roll(jnp.where(low[0:8], odd[0:8], even[0:8]), 64, 1)
    for t in range(TILES, SLABS):
        tiles_ref[t] = jnp.zeros((Q, 128), F32)


def pick_data(side, pick, freqs, tiles):
    row = lax.broadcasted_iota(jnp.int32, (8, 128), 0)
    recs = [(row // KC + 2 * g).astype(F32) for g in range(RK // 8)]
    for t in tiles:
        at = slice(t * 128, (t + 1) * 128)
        v = side[:, at]
        coef = 0.5 * jnp.where(row < KC, v, pltpu.roll(v, KC, 0))
        rec = jnp.broadcast_to(v[4:5], (8, 128))
        freqs[:, at] = jnp.broadcast_to(v[5:6], (8, 128))
        for g in range(RK // 16):
            two = [jnp.where(rec == recs[2 * g + i], coef, 0.0) for i in range(2)]
            pick[g * 16 : g * 16 + 16, at] = jnp.concatenate(two, axis=0).astype(BF)


def of_component(v, k):
    lane = lax.rem(lax.broadcasted_iota(jnp.int32, v.shape, 1), KC)
    return jnp.where(lane == k, v, 0.0)


def from_data(tiles, pick, freqs, z, v, prepare=lambda group: None):
    w = jnp.zeros((NFREQ * Q, RK), F32)
    for start in range(0, TILES, 6):
        group = range(start, start + 6)
        prepare(group)
        for t in group:
            at = slice(t * 128, (t + 1) * 128)
            x = tiles(t)
            freq = jnp.concatenate([freqs[:, at], freqs[:, at]], axis=0)
            for f in range(NFREQ):
                z[f * Q : (f + 1) * Q, at] = jnp.where(freq == float(f), x, 0.0).astype(BF)
        at = slice(start * 128, (start + 6) * 128)
        w = w + lax.dot_general(z[:, at], pick[:, at], NT, preferred_element_type=F32)
    for f in range(NFREQ):
        for k in range(KC):
            fk = f * KC + k
            v[fk * Q : (fk + 1) * Q, :] = of_component(w[f * Q : (f + 1) * Q], k).astype(BF)


def to_cells(v, basis, field):
    u = jnp.dot(v[...], basis, preferred_element_type=F32)
    total = [jnp.zeros((Q, u.shape[1]), F32) for _ in range(4)]
    for fk in range(FK):
        total[fk % 4] = total[fk % 4] + field(fk) * u[fk * Q : (fk + 1) * Q, :]
    return (total[0] + total[1]) + (total[2] + total[3])


def center_cells(v, adj_ref, field, cell):
    for i in range(CELLS // 256):
        at = slice(i * 256, (i + 1) * 256)
        cell[:, at] = to_cells(v, adj_ref[:, at], lambda fk: field[fk : fk + 1, at])


def with_edges(v, up_ref, down_ref, edge, cell):
    edge[:, 0:HALO] = up_ref[RK:, :].astype(F32)
    edge[:, HALO:] = down_ref[RK:, :].astype(F32)
    up = to_cells(v, up_ref[0:RK, :], lambda fk: edge[fk : fk + 1, 0:HALO])
    down = to_cells(v, down_ref[0:RK, :], lambda fk: edge[fk : fk + 1, HALO:])
    rows = [up[:, 0:COLS], up[:, COLS:]]
    rows += [cell[:, r * COLS : (r + 1) * COLS] for r in range(GRID_ROWS)]
    rows += [down[:, 0:COLS], down[:, COLS:]]
    j = lax.axis_index("mp")
    return smooth_rows(rows, j == 0, j == SLABS - 1)


def back_kernel(recv_ref, adj_ref, fwd_ref, pick, freqs, tiles_ref, v, field, cell, z, side):
    unpack(recv_ref, tiles_ref, side)
    field[...] = fwd_ref[...].astype(F32)
    from_data(lambda t: tiles_ref[t], pick, freqs, z, v, lambda group: pick_data(side, pick, freqs, group))
    center_cells(v, adj_ref, field, cell)


def gram_kernel(v, cell_ref, pick, freqs, field, adj_ref, up_ref, down_ref, gram_ref, edge, z, y):
    rows = with_edges(v, up_ref, down_ref, edge, cell_ref)
    for r in range(GRID_ROWS):
        at = slice(r * COLS, (r + 1) * COLS)
        x = rows[r] * (1.0 / (CELLS * SLABS))
        for fk in range(FK):
            z[fk * Q : (fk + 1) * Q, at] = (field[fk : fk + 1, at] * x).astype(BF)
    w = lax.dot_general(z[...], adj_ref[...], NT, preferred_element_type=F32)
    for f in range(NFREQ):
        part = [of_component(w[(f * KC + k) * Q : (f * KC + k + 1) * Q], k) for k in range(KC)]
        y[f * Q : (f + 1) * Q, :] = ((part[0] + part[1]) + (part[2] + part[3])).astype(BF)
    for i in range(TILES // 2):
        at = slice(i * 256, (i + 1) * 256)
        u = jnp.dot(y[...], pick[:, at], preferred_element_type=F32)
        freq = jnp.concatenate([freqs[:, at], freqs[:, at]], axis=0)
        g = jnp.zeros((Q, 256), F32)
        for f in range(NFREQ):
            g = jnp.where(freq == float(f), u[f * Q : (f + 1) * Q], g)
        gram_ref[2 * i] = g[:, 0:128].astype(BF)
        gram_ref[2 * i + 1] = g[:, 128:256].astype(BF)


def smooth_rows(rows, first, last):
    lane = lax.broadcasted_iota(jnp.int32, (Q, COLS), 1)

    def sweep(rows):
        out = []
        for i in range(1, len(rows) - 1):
            x = rows[i]
            left = jnp.where(lane == 0, 0.0, pltpu.roll(x, 1, 1))
            right = jnp.where(lane == COLS - 1, 0.0, pltpu.roll(x, COLS - 1, 1))
            out.append(x + 0.2 * ((rows[i - 1] + rows[i + 1] + left + right) - 4.0 * x))
        return out

    once = sweep(rows)
    once[0] = once[0] * jnp.where(first, 0.0, 1.0)
    once[-1] = once[-1] * jnp.where(last, 0.0, 1.0)
    return sweep(once)


def update_kernel(parts_ref, out_ref):
    total = parts_ref[0].astype(F32)
    for z in range(1, 8):
        total = total + parts_ref[z].astype(F32)
    total = total.astype(BF)
    for j in range(SLABS):
        out_ref[j] = total


def model_kernel(sums_ref, tiles_ref, pick, freqs, field, adj_ref, up_ref, down_ref, out_ref, z, v, cell, edge, upd_ref):
    for t in range(TILES):
        at = slice((t % 3) * Q, (t % 3 + 1) * Q)
        part = [sums_ref[(t // 3) * 4 + y, at, :].astype(F32) for y in range(4)]
        upd_ref[t] = (((part[0] + part[1]) + (part[2] + part[3])) + tiles_ref[t]).astype(BF).astype(F32)
    from_data(lambda t: upd_ref[t], pick, freqs, z, v)
    center_cells(v, adj_ref, field, cell)
    rows = with_edges(v, up_ref, down_ref, edge, cell)
    low = lax.broadcasted_iota(jnp.int32, (8, 128), 1) < 64
    for b in range(BLOCKS):
        tail = upd_ref[BLOCKS + b // 2]
        turned = pltpu.roll(tail, 64, 1)
        tail = jnp.where(low, tail[0:8], turned[8:16]) if b % 2 == 0 else jnp.where(low, turned[0:8], tail[8:16])
        piece = [rows[b] * (1.0 / math.sqrt(NDATA)), upd_ref[b], tail]
        out_ref[b] = jnp.concatenate(piece, axis=0).astype(BF)


def finish_kernel(recv_ref, upd_ref, model_ref):
    pieces = [recv_ref[b].astype(F32) for b in range(BLOCKS)]
    model_ref[...] = jnp.transpose(jnp.concatenate([p[0:Q] for p in pieces], axis=0))
    upd_ref[0:128, :] = jnp.transpose(jnp.concatenate([p[Q : 2 * Q] for p in pieces], axis=0)).astype(BF)
    tail = []
    for p in pieces:
        tail += [p[2 * Q :], pltpu.roll(p[2 * Q :], 64, 1)]
    upd_ref[128:DATA, :] = jnp.transpose(jnp.concatenate(tail, axis=0))[0:64].astype(BF)


def per_device(forward_fields, adjoint_fields, data_rec, data_freq, data_coef, residual_cols):
    shape = jax.ShapeDtypeStruct
    params = pltpu.CompilerParams(vmem_limit_bytes=40 * 1024 * 1024)
    call = functools.partial(pl.pallas_call, compiler_params=params)
    adj = adjoint_fields.reshape(RK, CELLS)
    fwd = forward_fields.reshape(FK, CELLS)
    send_down = jnp.concatenate([adj[:, -HALO:], fwd[:, -HALO:]], axis=0)
    send_up = jnp.concatenate([adj[:, :HALO], fwd[:, :HALO]], axis=0)
    to_next = [
        (j * BLOCKS + i, (j + 1) * BLOCKS + (i ^ 2 if j % 4 == 3 else i)) for j in range(SLABS - 1) for i in range(BLOCKS)
    ]
    up = lax.ppermute(send_down, ("mp", "dp"), to_next)
    down = lax.ppermute(send_up, ("mp", "dp"), [(b, a) for a, b in to_next])
    packed = pl.pallas_call(
        pack_kernel,
        compiler_params=pltpu.CompilerParams(vmem_limit_bytes=60 * 1024 * 1024),
        out_shape=shape((BLOCKS, 2 * Q + 8, 128), BF),
        in_specs=[pl.BlockSpec(memory_space=pl.ANY)] * 4,
        out_specs=whole(1)[0],
        scratch_shapes=[
            pltpu.VMEM((DATA, RHS), BF),
            pltpu.VMEM((KC, DATA), F32),
            pltpu.VMEM((1, DATA), jnp.int32),
            pltpu.VMEM((1, DATA), jnp.int32),
            pltpu.SemaphoreType.DMA((4,)),
            pltpu.VMEM((256, RHS), F32),
            pltpu.VMEM((8, 256), F32),
        ],
    )(residual_cols, data_coef.T, data_rec.reshape(1, DATA), data_freq.reshape(1, DATA))
    recv = lax.all_to_all(packed, ("mp", "dp"), 0, 0, axis_index_groups=NEAR)
    pick, freqs, tiles, v, field, cell = call(
        back_kernel,
        out_shape=[
            shape((RK, NDATA), BF),
            shape((8, NDATA), F32),
            shape((SLABS, Q, 128), F32),
            shape((FK * Q, RK), BF),
            shape((FK, CELLS), F32),
            shape((Q, CELLS), F32),
        ],
        in_specs=whole(3),
        out_specs=whole(6),
        scratch_shapes=[pltpu.VMEM((NFREQ * Q, NDATA), BF), pltpu.VMEM((8, NDATA), F32)],
        cost_estimate=pl.CostEstimate(flops=4 * 10**9, bytes_accessed=8 * 10**6, transcendentals=0),
    )(recv, adj, fwd)
    gram = call(
        gram_kernel,
        out_shape=shape((TILES, Q, 128), BF),
        in_specs=whole(8),
        out_specs=whole(1)[0],
        scratch_shapes=[
            pltpu.VMEM((FK, 2 * HALO), F32),
            pltpu.VMEM((FK * Q, CELLS), BF),
            pltpu.VMEM((NFREQ * Q, RK), BF),
        ],
    )(v, cell, pick, freqs, field, adj, up, down)
    parts = lax.all_to_all(gram.reshape(8, 3 * Q, 128), "mp", 0, 0, axis_index_groups=ALONG_Z)
    mine = call(update_kernel, out_shape=shape((SLABS, 3 * Q, 128), BF), in_specs=whole(1), out_specs=whole(1)[0])(parts)
    update = lax.all_to_all(mine, "mp", 0, 0)
    rows = call(
        model_kernel,
        out_shape=shape((BLOCKS, 2 * Q + 8, 128), BF),
        in_specs=whole(8),
        out_specs=whole(1)[0],
        scratch_shapes=[
            pltpu.VMEM((NFREQ * Q, NDATA), BF),
            pltpu.VMEM((FK * Q, RK), BF),
            pltpu.VMEM((Q, CELLS), F32),
            pltpu.VMEM((FK, 2 * HALO), F32),
            pltpu.VMEM((TILES, Q, 128), F32),
        ],
    )(update, tiles, pick, freqs, field, adj, up, down)
    last = lax.all_to_all(rows, "dp", 0, 0)
    return call(
        finish_kernel,
        out_shape=[shape((DATA, RHS), BF), shape((COLS, RHS), F32)],
        in_specs=whole(1),
        out_specs=whole(2),
    )(last)


def solution(mesh):
    in_specs = (
        P(None, None, "mp"),
        P(None, None, "mp"),
        P("dp"),
        P("dp"),
        P("dp", None),
        P("dp", None),
    )
    out_specs = (P("dp", None), P(("mp", "dp"), None))
    return jax.shard_map(
        per_device, mesh=mesh, in_specs=in_specs, out_specs=out_specs, check_vma=False
    )
```
